32 devices in a mesh: ctx: 8 (over z, x), head: 4 (over y, core).
Axes of the slice: x: 2, y: 2, z: 4, core: 2. Of those that a mesh axis runs over, the one named last changes fastest.
Arguments:
- lin_query: bfloat16 [3072, 8192], P('ctx', 'head'), may hold values from -4 to 4
- lin_key: bfloat16 [3072, 8192], P('ctx', 'head'), may hold values from -4 to 4
- lin_value: bfloat16 [3072, 8192], P('ctx', 'head'), may hold values from -400 to 400
- lin_gate: bfloat16 [3072, 8192], P('ctx', 'head'), may hold values from -8 to 8
- lin_decay: float32 [3072, 64], P('ctx', 'head'), may hold values from -1 to 0
- norm_gain: float32 [8192], P('head'), may hold values from 0.25 to 1.75
- soft_query: bfloat16 [3072, 8192], P('ctx', 'head'), may hold values from -6.5 to 6.5
- soft_key: bfloat16 [3072, 1024], P('ctx', 'head'), may hold values from -6.5 to 6.5
- soft_value: bfloat16 [3072, 1024], P('ctx', 'head'), may hold values from -6 to 6
- starts: int32 [4], replicated, may hold values from 1 to 2400, as said below
- lengths: int32 [4], replicated, may hold values from 384 to 768, as said below
Outputs:
- lin_out: bfloat16 [3072, 8192], P('ctx', 'head')
- soft_out: bfloat16 [3072, 8192], P('ctx', 'head')
The draws below stay inside these ranges and needn't reach their ends.
Inputs may be any that keep to these rules, and one draw needn't show every extreme that they name: `starts`: sequence s begins 1 to min(96, 192) positions after s * 768; sequences 1 and 2 begin at the same offset, no sequence runs into the next, and the last one ends at the pack's end. `lengths`: sequence 1 has length 768 in every draw.
All inputs are finite; a program needn't handle non-finite values.
Results may differ from the reference program's by a relative error of at most 0.012.
Values may be sent and summed in bfloat16 or wider, within the bound.
A program may use at most 128 MiB of HBM per device.

```python
import math
import jax
import jax.numpy as jnp
from jax import lax

HEADS = 64
HD = 128
KV_HEADS = 8
TOK_DEV = 384
SEQS = 4
WIDTH = 8192
KV_WIDTH = 1024
PACK_LENGTH = 3072
SEQUENCE_ROOM = 768
KEY_SPAN = 1152


def sequence_bounds(key):
    floor_level = jax.random.fold_in(key, 29)
    key_offset, key_length = jax.random.split(floor_level, 2)
    slot_ids = jnp.arange(SEQS, dtype=jnp.int32)
    top_offset = min(SEQUENCE_ROOM // 8, TOK_DEV // 2)
    offsets = jax.random.randint(key_offset, (SEQS,), 1, top_offset + 1)
    offsets = jnp.where(slot_ids == 2, offsets[1], offsets)
    first = slot_ids * SEQUENCE_ROOM + offsets
    following = jnp.concatenate([first[1:], jnp.array([PACK_LENGTH], dtype=jnp.int32)])
    room_left = following - first
    length_top = jnp.minimum(room_left, SEQUENCE_ROOM)
    chosen = jax.random.randint(key_length, (SEQS,), SEQUENCE_ROOM // 2, length_top + 1)
    chosen = jnp.where(slot_ids == 1, SEQUENCE_ROOM, chosen)
    chosen = jnp.where(slot_ids == SEQS - 1, room_left, chosen)
    return (first.astype(jnp.int32), chosen.astype(jnp.int32))


def draw_starts(key, part):
    first, unused = sequence_bounds(key)
    return first


def draw_lengths(key, part):
    unused, chosen = sequence_bounds(key)
    return chosen


def draw_lin_decay(key, part):
    floor_level = jax.random.fold_in(key, 3)
    quick_seed, speed_seed, gradual_seed, noise_seed, spike_seed, drop_seed = jax.random.split(floor_level, 6)
    fast_share = 0.5
    fast = jax.random.uniform(quick_seed, (HEADS,)) < fast_share
    fast_rate = jnp.exp(jax.random.uniform(speed_seed, (HEADS,), minval=math.log(0.05), maxval=math.log(0.1)))
    slow_rate = jnp.exp(jax.random.uniform(gradual_seed, (HEADS,), minval=math.log(0.05), maxval=math.log(0.5))) / SEQUENCE_ROOM
    forget_factor = jnp.where(fast, fast_rate, slow_rate)
    noise_size = jax.random.uniform(noise_seed, (PACK_LENGTH, HEADS), minval=0.5, maxval=1.5)
    spike_size = jax.random.randint(spike_seed, (PACK_LENGTH, 1), 0, SEQUENCE_ROOM // 2) == 0
    drop_size = jax.random.uniform(drop_seed, (PACK_LENGTH, HEADS), minval=0.2, maxval=0.5)
    element_item = -forget_factor[None, :] * noise_size + jnp.where(spike_size, jnp.log(1.0 - drop_size), 0.0)
    return element_item.astype(jnp.float32)


def draw_lin_value(key, part):
    floor_level = jax.random.fold_in(key, 5)
    key_base, key_column, key_row = jax.random.split(floor_level, 3)
    features = HEADS * HD
    head_of = (jnp.arange(features) // HD).astype(jnp.float32)
    ramp = jnp.power(3.0, head_of / max(HEADS - 1, 1))
    column_scale = ramp * jnp.exp(jax.random.uniform(key_column, (features,), minval=0.0, maxval=math.log(3.3)))
    entries = jnp.clip(jax.random.normal(key_base, (PACK_LENGTH, features)), -4.0, 4.0)
    row_scale = jnp.exp(jax.random.uniform(key_row, (PACK_LENGTH, 1), minval=0.0, maxval=math.log(10.0)))
    return (entries * column_scale[None, :] * row_scale).astype(jnp.bfloat16)


def soft_pair(key):
    floor_level = jax.random.fold_in(key, 17)
    key_query, key_key = jax.random.split(floor_level, 2)
    features = HEADS * HD
    kv_features = KV_HEADS * HD
    queries = jnp.clip(jax.random.normal(key_query, (PACK_LENGTH, features)), -4.0, 4.0)
    keys = jnp.clip(jax.random.normal(key_key, (PACK_LENGTH, kv_features)), -4.0, 4.0)
    return (queries, keys)


def draw_soft_query(key, part):
    queries, keys = soft_pair(key)
    return queries.astype(jnp.bfloat16)


def draw_soft_key(key, part):
    queries, keys = soft_pair(key)
    return keys.astype(jnp.bfloat16)


def shard_levels(key, extent, cuts, low, top_value):
    level, own = 1.0, jax.random.fold_in(key, 6)
    for position, shards_of in cuts:
        heights = jnp.exp(jax.random.uniform(jax.random.fold_in(own, position), (shards_of,), jnp.float32, low / len(cuts), top_value / len(cuts)))
        level = level * jnp.repeat(heights, extent[position] // shards_of).reshape([-1 if axis == position else 1 for axis in range(len(extent))])
    return level


def noise(rng, extent, scale, most, shards=(), kind=jnp.bfloat16):
    values = jax.random.normal(rng, extent, jnp.float32) * scale
    if len(shards) > 0:
        values = shard_levels(rng, extent, shards, -0.22, 0.18) * values
    return jnp.clip(values, min=-most, max=most).astype(kind)


def setup_inputs(seed: int = 0) -> dict:
    seeds = jax.random.split(jax.random.key(seed), 12)
    lin_query = noise(seeds[0], (PACK_LENGTH, WIDTH), 1.0, 4.0, ((0, 8), (1, 4)))
    lin_key = noise(seeds[1], (PACK_LENGTH, WIDTH), 1.0, 4.0, ((0, 8), (1, 4)))
    lin_value = draw_lin_value(jax.random.fold_in(seeds[11], 71), 0)
    lin_gate = noise(seeds[3], (PACK_LENGTH, WIDTH), 2.0, 8.0, ((0, 8), (1, 4)))
    lin_decay = draw_lin_decay(jax.random.fold_in(seeds[11], 71), 0)
    norm_gain = jnp.clip(1.0 + 0.15 * jax.random.normal(seeds[5], (WIDTH,), jnp.float32), 0.25, 1.75)
    soft_query = draw_soft_query(jax.random.fold_in(seeds[11], 71), 0)
    soft_key = draw_soft_key(jax.random.fold_in(seeds[11], 71), 0)
    soft_value = noise(seeds[8], (PACK_LENGTH, KV_WIDTH), 1.0, 6.0, ((0, 8), (1, 4)))
    starts = draw_starts(jax.random.fold_in(seeds[11], 71), 0)
    lengths = draw_lengths(jax.random.fold_in(seeds[11], 71), 0)
    return {"lin_query": lin_query, "lin_key": lin_key, "lin_value": lin_value, "lin_gate": lin_gate, "lin_decay": lin_decay, "norm_gain": norm_gain, "soft_query": soft_query, "soft_key": soft_key, "soft_value": soft_value, "starts": starts, "lengths": lengths}


neg_big = -1e+30
norm_eps = 1e-06

def segment_info(positions, starts, lengths):
    begun = (starts[None, :] <= positions[:, None]).astype(jnp.int32)
    segment = lax.optimization_barrier(jnp.sum(begun, axis=1)) - 1
    picked = jnp.arange(starts.shape[0], dtype=jnp.int32)[None, :] == segment[:, None]
    seg_start = lax.optimization_barrier(jnp.sum(jnp.where(picked, starts[None, :], 0), axis=1))
    seg_length = lax.optimization_barrier(jnp.sum(jnp.where(picked, lengths[None, :], 0), axis=1))
    valid = (segment >= 0) & (positions < seg_start + seg_length)
    return (segment, valid)

def lightning_local(query, keys, values, decay, segment, valid, before):
    row_count = query.shape[0]
    cumulative = jnp.cumsum(decay, axis=0)
    row_order = jnp.arange(row_count)
    visible = (row_order[None, :] <= row_order[:, None]) & (segment[None, :] == segment[:, None]) & valid[None, :]
    by_head = jnp.transpose(cumulative)
    log_gap = by_head[:, :, None] - by_head[:, None, :]
    factor = jnp.where(visible[None], jnp.exp(jnp.where(visible[None], log_gap, 0.0)), 0.0)
    scores = jnp.einsum('thd,shd->hts', query.astype(jnp.float32), keys.astype(jnp.float32), precision=lax.Precision.HIGHEST)
    weights = (scores * factor).astype(jnp.bfloat16)
    intra = jnp.einsum('hts,shd->thd', weights.astype(jnp.float32), values.astype(jnp.float32), precision=lax.Precision.HIGHEST)
    enter = jnp.exp(cumulative) * (segment == before).astype(jnp.float32)[:, None]
    end_ok = ((segment == segment[-1]) & valid).astype(jnp.float32)
    to_end = jnp.exp(cumulative[-1][None, :] - cumulative) * end_ok[:, None]
    decay_total = jnp.exp(cumulative[-1]) * (segment[-1] == before).astype(jnp.float32)
    local_state = jnp.einsum('thd,the->hde', keys.astype(jnp.float32) * to_end[:, :, None], values.astype(jnp.float32), precision=lax.Precision.HIGHEST)
    return (intra, enter, decay_total, local_state)

def reference(lin_query, lin_key, lin_value, lin_gate, lin_decay, norm_gain, soft_query, soft_key, soft_value, starts, lengths):
    blocks = PACK_LENGTH // TOK_DEV
    group = HEADS // KV_HEADS

    def blocked(array):
        return array.reshape(blocks, TOK_DEV, HEADS, HD)

    def lightning_step(state, inputs):
        block_index, query, keys, values, decay = inputs
        first = block_index * TOK_DEV
        positions = first + jnp.arange(TOK_DEV, dtype=jnp.int32)
        segment, valid = segment_info(positions, starts, lengths)
        before, unused = segment_info(jnp.reshape(first - 1, (1,)), starts, lengths)
        intra, enter, decay_total, local_state = lightning_local(query, keys, values, decay, segment, valid, before[0])
        carried = jnp.einsum('thd,hde->the', query.astype(jnp.float32) * enter[:, :, None], state, precision=lax.Precision.HIGHEST)
        heads_out = (intra + carried) * valid.astype(jnp.float32)[:, None, None]
        new_state = decay_total[:, None, None] * state + local_state
        return (new_state, heads_out)
    initial = jnp.zeros((HEADS, HD, HD), jnp.float32)
    indices = jnp.arange(blocks, dtype=jnp.int32)
    decays = lin_decay.reshape(blocks, TOK_DEV, HEADS)
    unused_state, lin_heads = lax.scan(lightning_step, initial, (indices, blocked(lin_query), blocked(lin_key), blocked(lin_value), decays))
    flat = lin_heads.reshape(PACK_LENGTH, HEADS * HD)
    mean_square = lax.optimization_barrier(jnp.mean(flat * flat, axis=1))
    lin_out = (flat * lax.rsqrt(mean_square + norm_eps)[:, None] * norm_gain[None, :] * jax.nn.sigmoid(lin_gate.astype(jnp.float32))).astype(jnp.bfloat16)
    positions_all = jnp.arange(PACK_LENGTH, dtype=jnp.int32)
    seg_all, valid_all = segment_info(positions_all, starts, lengths)
    score_scale = HD ** (-0.5)
    query_heads = jnp.transpose(soft_query.reshape(PACK_LENGTH, KV_HEADS, group, HD), (1, 2, 0, 3))
    key_heads = jnp.transpose(soft_key.reshape(PACK_LENGTH, KV_HEADS, HD), (1, 0, 2))
    value_heads = jnp.transpose(soft_value.reshape(PACK_LENGTH, KV_HEADS, HD), (1, 0, 2))

    def soft_block(block_index):
        first = (block_index * TOK_DEV).astype(jnp.int32)
        key_first = jnp.clip(first - SEQUENCE_ROOM, 0, PACK_LENGTH - KEY_SPAN).astype(jnp.int32)
        query_seg = lax.dynamic_slice_in_dim(seg_all, first, TOK_DEV, 0)
        query_valid = lax.dynamic_slice_in_dim(valid_all, first, TOK_DEV, 0)
        key_seg = lax.dynamic_slice_in_dim(seg_all, key_first, KEY_SPAN, 0)
        key_valid = lax.dynamic_slice_in_dim(valid_all, key_first, KEY_SPAN, 0)
        query_pos = first + jnp.arange(TOK_DEV, dtype=jnp.int32)
        key_pos = key_first + jnp.arange(KEY_SPAN, dtype=jnp.int32)
        visible = (key_pos[None, :] <= query_pos[:, None]) & (key_seg[None, :] == query_seg[:, None]) & key_valid[None, :]
        query_block = lax.dynamic_slice_in_dim(query_heads, first, TOK_DEV, 2)
        key_block = lax.dynamic_slice_in_dim(key_heads, key_first, KEY_SPAN, 1)
        value_block = lax.dynamic_slice_in_dim(value_heads, key_first, KEY_SPAN, 1)

        def one_head(operands):
            query_one, key_one, value_one = operands
            scores = jnp.einsum('gqd,sd->gqs', query_one.astype(jnp.float32), key_one.astype(jnp.float32), precision=lax.Precision.HIGHEST) * score_scale
            masked = jnp.where(visible[None], scores, neg_big)
            peak = lax.optimization_barrier(jnp.max(masked, axis=2, keepdims=True))
            probs = jnp.where(visible[None], jnp.exp(masked - peak), 0.0)
            totals = lax.optimization_barrier(jnp.sum(probs, axis=2, keepdims=True))
            mixed = jnp.einsum('gqs,sd->gqd', probs.astype(jnp.bfloat16).astype(jnp.float32), value_one.astype(jnp.float32), precision=lax.Precision.HIGHEST)
            safe = jnp.where(query_valid[None, :, None], totals, 1.0)
            return (mixed / safe * query_valid.astype(jnp.float32)[None, :, None]).astype(jnp.bfloat16)
        return lax.map(one_head, (query_block, key_block, value_block))
    soft_heads = lax.map(soft_block, jnp.arange(blocks, dtype=jnp.int32))
    soft_out = jnp.transpose(soft_heads, (0, 3, 1, 2, 4)).reshape(PACK_LENGTH, HEADS * HD)
    return (lin_out, soft_out)
```

```python
import functools

import jax
import jax.numpy as jnp
from jax import lax
from jax.experimental import pallas as pl
from jax.experimental.pallas import tpu as pltpu
from jax.sharding import PartitionSpec as P

neg_big = -1e30
norm_eps = 1e-06
MESH = pl.DeviceIdType.MESH
TILE = 128
PARTS = 4


def dot_rows(a, b):
    return lax.dot_general(a, b, (((1,), (1,)), ((), ())), preferred_element_type=jnp.float32)


def dot_plain(a, b):
    return jnp.dot(a, b, preferred_element_type=jnp.float32)


def kernel(
    ctx_size,
    head_size,
    lq_hbm,
    lk_hbm,
    lv_hbm,
    gate_hbm,
    decay_ref,
    gain_ref,
    sq_hbm,
    sk_hbm,
    sv_hbm,
    starts_ref,
    lengths_ref,
    lin_hbm,
    soft_hbm,
    lq,
    lk,
    lv,
    gate,
    sq,
    sk,
    sv,
    far_k,
    far_v,
    state_mine,
    state_far,
    total_mine,
    total_far,
    decay_pad,
    c_row,
    c_all,
    enter_all,
    end_all,
    valid_col,
    bias,
    lin,
    peak,
    total,
    acc,
    square_mine,
    square_far,
    lin_stage,
    soft_stage,
    in_sem,
    out_sem,
    kv_send,
    kv_recv,
    state_send,
    state_recv,
    square_send,
    square_recv,
):
    rows, features = lq.shape
    heads = features // TILE
    kv_count = sk.shape[1] // TILE
    group = heads // kv_count
    seqs = starts_ref.shape[0]
    window = ctx_size // seqs
    row_tiles = rows // TILE
    reach = min(window * rows // 8, rows // 2)
    head_rows = -(-reach // TILE) * TILE
    me = lax.axis_index("ctx")
    mine = lax.axis_index("head")
    place = lax.rem(me, window)
    first = me * rows
    opening = place == 0

    loads = [
        pltpu.make_async_copy(source, target, in_sem.at[i])
        for i, (source, target) in enumerate(
            ((lk_hbm, lk), (lv_hbm, lv), (lq_hbm, lq), (sk_hbm, sk), (sv_hbm, sv), (sq_hbm, sq), (gate_hbm, gate))
        )
    ]
    for load in loads:
        load.start()

    def receives(distance):
        return (opening & (me > 0)) | (place >= distance)

    def sends(distance):
        target = lax.rem(me + distance, window)
        return (me + distance < ctx_size) & ((target == 0) | (target >= distance))

    barrier = pltpu.get_barrier_semaphore()
    for distance in range(1, window + 1):

        @pl.when(receives(distance))
        def greet_source():
            pl.semaphore_signal(barrier, inc=1, device_id={"ctx": me - distance}, device_id_type=MESH)

        @pl.when(sends(distance))
        def greet_target():
            pl.semaphore_signal(barrier, inc=1, device_id={"ctx": me + distance}, device_id_type=MESH)

    for step in range(1, head_size):
        peer = lax.rem(mine + step, head_size)
        pl.semaphore_signal(barrier, inc=1, device_id={"head": peer}, device_id_type=MESH)

    def segment_of(pos):
        segment = jnp.full(pos.shape, -1, jnp.int32)
        for s in range(seqs):
            segment = segment + jnp.where(starts_ref[s] <= pos, 1, 0)
        stop = jnp.zeros(pos.shape, jnp.int32)
        for s in range(seqs):
            stop = jnp.where(segment == s, starts_ref[s] + lengths_ref[s], stop)
        return segment, (segment >= 0) & (pos < stop)

    def segment_at(pos):
        segment = jnp.int32(-1)
        for s in range(seqs):
            segment = segment + jnp.where(starts_ref[s] <= pos, 1, 0)
        return segment

    before = segment_at(first - 1)
    last = segment_at(first + rows - 1)
    row_pos = lax.broadcasted_iota(jnp.int32, (rows, TILE), 0) + first
    row_seg, row_valid = segment_of(row_pos)
    valid_col[...] = row_valid.astype(jnp.float32)

    def key_code(owner):
        pos = lax.broadcasted_iota(jnp.int32, (8, rows), 1) + owner * rows
        segment, valid = segment_of(pos)
        return jnp.where(valid, segment, -7)[0:1]

    query_seg = row_seg[:, 0:1]
    own_code = key_code(me)
    order = lax.broadcasted_iota(jnp.int32, (rows, rows), 1) <= lax.broadcasted_iota(
        jnp.int32, (rows, rows), 0
    )
    bias[0] = jnp.where(order & (query_seg == own_code), 0.0, neg_big)
    for distance in range(1, window + 1):
        bias[distance] = jnp.where(query_seg == key_code(me - distance), 0.0, neg_big)

    decay_pad[...] = jnp.zeros_like(decay_pad)
    decay_pad[:, 0:heads] = decay_ref[...]
    lower = jnp.where(order, 1.0, 0.0)
    cumulative = lax.dot_general(
        lower,
        decay_pad[...],
        (((1,), (0,)), ((), ())),
        precision=lax.Precision.HIGHEST,
        preferred_element_type=jnp.float32,
    )
    c_all[...] = cumulative
    by_head = cumulative.T
    c_row[...] = by_head
    enter_all[...] = jnp.where(row_seg == before, jnp.exp(cumulative), 0.0)
    end_all[...] = jnp.where(
        (row_seg == last) & row_valid, jnp.exp(cumulative[rows - 1 : rows] - cumulative), 0.0
    )
    whole = jnp.exp(by_head[0:heads, rows - 1 : rows]) * jnp.where(last == before, 1.0, 0.0)
    total_mine[...] = jnp.broadcast_to(whole, (heads, TILE))

    greetings = head_size - 1
    for distance in range(1, window + 1):
        greetings = greetings + jnp.where(receives(distance), 1, 0)
        greetings = greetings + jnp.where(sends(distance), 1, 0)
    pl.semaphore_wait(barrier, greetings)

    def total_copy(distance):
        return pltpu.make_async_remote_copy(
            src_ref=total_mine,
            dst_ref=total_far.at[distance - 1],
            send_sem=state_send.at[distance - 1, PARTS],
            recv_sem=state_recv.at[distance - 1, PARTS],
            device_id={"ctx": me + distance},
            device_id_type=MESH,
        )

    share = heads // PARTS

    def state_copy(distance, part):
        span = pl.ds(part * share, share)
        return pltpu.make_async_remote_copy(
            src_ref=state_mine.at[span],
            dst_ref=state_far.at[distance - 1, span],
            send_sem=state_send.at[distance - 1, part],
            recv_sem=state_recv.at[distance - 1, part],
            device_id={"ctx": me + distance},
            device_id_type=MESH,
        )

    def kv_copies(distance):
        return [
            pltpu.make_async_remote_copy(
                src_ref=source,
                dst_ref=target.at[distance - 1],
                send_sem=kv_send.at[distance - 1, i],
                recv_sem=kv_recv.at[distance - 1, i],
                device_id={"ctx": me + distance},
                device_id_type=MESH,
            )
            for i, (source, target) in enumerate(((sk_hbm, far_k), (sv_hbm, far_v)))
        ]

    def far_copies(distance):
        return (
            [total_copy(distance)]
            + [state_copy(distance, part) for part in range(PARTS)]
            + kv_copies(distance)
        )

    def lanes(head):
        return pl.ds(pl.multiple_of(head * TILE, TILE), TILE)

    lane_id = lax.broadcasted_iota(jnp.int32, (rows, TILE), 1)

    def column(ref, head):
        return jnp.sum(jnp.where(lane_id == head, ref[...], 0.0), axis=1, keepdims=True)

    loads[0].wait()
    loads[1].wait()

    def make_state(head, carry):
        scaled = (lk[:, lanes(head)].astype(jnp.float32) * column(end_all, head)).astype(jnp.bfloat16)
        local = lax.dot_general(
            scaled, lv[:, lanes(head)], (((0,), (0,)), ((), ())), preferred_element_type=jnp.float32
        )
        state_mine[head] = local.astype(jnp.bfloat16)
        return carry

    for part in range(PARTS):
        lax.fori_loop(part * share, (part + 1) * share, make_state, 0)
        for distance in range(1, window + 1):

            @pl.when(sends(distance))
            def send_state():
                if part == 0:
                    total_copy(distance).start()
                state_copy(distance, part).start()

    for distance in range(1, window + 1):

        @pl.when(sends(distance))
        def send_keys():
            for copy in kv_copies(distance):
                copy.start()

    for load in loads[2:6]:
        load.wait()
    score_scale = TILE ** (-0.5)

    def within(head, carry):
        c_col = column(c_all, head)
        c_line = c_row[pl.ds(head, 1), :]
        span = lanes(head)
        kv_span = lanes(head // group)
        for tile in range(row_tiles):
            at = slice(tile * TILE, (tile + 1) * TILE)
            wide = (tile + 1) * TILE
            hidden = bias[0, at, 0:wide]
            factor = jnp.exp(c_col[at] - c_line[:, 0:wide] + hidden)
            weights = (dot_rows(lq[at, span], lk[0:wide, span]) * factor).astype(jnp.bfloat16)
            lin[at, span] = dot_plain(weights, lv[0:wide, span])
            scores = dot_rows(sq[at, span], sk[0:wide, kv_span]) * score_scale + hidden
            top = jnp.max(scores, axis=1, keepdims=True)
            probs = jnp.exp(scores - top)
            peak[head, at, :] = jnp.broadcast_to(top, (TILE, TILE))
            total[head, at, :] = jnp.broadcast_to(jnp.sum(probs, axis=1, keepdims=True), (TILE, TILE))
            acc[at, span] = dot_plain(probs.astype(jnp.bfloat16), sv[0:wide, kv_span])
        return carry

    lax.fori_loop(0, heads, within, 0)

    for distance in range(1, window + 1):

        @pl.when(receives(distance))
        def await_state():
            total_copy(distance).wait_recv()
            for part in range(PARTS):
                state_copy(distance, part).wait_recv()

    def carried_over(count, distances):
        def body(head, carry):
            state = state_far[0, head].astype(jnp.float32)
            if distances > 1:
                scale = total_far[0, pl.ds(head, 1), :]
                for index in range(1, distances):
                    state = state + scale * state_far[index, head].astype(jnp.float32)
                    scale = scale * total_far[index, pl.ds(head, 1), :]
            enter = column(enter_all, head)[0:count]
            span = lanes(head)
            lin[0:count, span] += enter * dot_plain(lq[0:count, span], state.astype(jnp.bfloat16))
            return carry

        lax.fori_loop(0, heads, body, 0)

    @pl.when(opening & (me > 0))
    def carry_opening():
        carried_over(head_rows, window)

    for distance in range(1, window):

        @pl.when(place == distance)
        def carry_inside():
            carried_over(rows, distance)

    def square(head, so_far):
        value = lin[:, lanes(head)] * valid_col[...]
        return so_far + value * value

    squares = lax.fori_loop(0, heads, square, jnp.zeros((rows, TILE), jnp.float32))
    square_mine[...] = lax.dot_general(
        jnp.ones((8, TILE), jnp.float32),
        squares,
        (((1,), (1,)), ((), ())),
        precision=lax.Precision.HIGHEST,
        preferred_element_type=jnp.float32,
    )

    def square_copy(step):
        return pltpu.make_async_remote_copy(
            src_ref=square_mine,
            dst_ref=square_far.at[step - 1],
            send_sem=square_send.at[step - 1],
            recv_sem=square_recv.at[step - 1],
            device_id={"head": lax.rem(mine + step, head_size)},
            device_id_type=MESH,
        )

    for step in range(1, head_size):
        square_copy(step).start()

    for distance in range(1, window + 1):

        @pl.when(receives(distance))
        def await_keys():
            for copy in kv_copies(distance):
                copy.wait_recv()

    def attend_far(count, distances):
        def body(head, carry):
            span = lanes(head)
            kv_span = lanes(head // group)
            for tile in range(count // TILE):
                at = slice(tile * TILE, (tile + 1) * TILE)
                top = peak[head, at, :][:, 0:1]
                sums = total[head, at, :][:, 0:1]
                mixed = acc[at, span]
                query = sq[at, span]
                for index in range(distances):
                    scores = dot_rows(query, far_k[index, :, kv_span]) * score_scale
                    scores = scores + bias[index + 1, at, :]
                    higher = jnp.maximum(top, jnp.max(scores, axis=1, keepdims=True))
                    shrink = jnp.exp(top - higher)
                    probs = jnp.exp(scores - higher)
                    sums = sums * shrink + jnp.sum(probs, axis=1, keepdims=True)
                    mixed = mixed * shrink + dot_plain(
                        probs.astype(jnp.bfloat16), far_v[index, :, kv_span]
                    )
                    top = higher
                total[head, at, :] = jnp.broadcast_to(sums, (TILE, TILE))
                acc[at, span] = mixed
            return carry

        lax.fori_loop(0, heads, body, 0)

    @pl.when(opening & (me > 0))
    def attend_opening():
        attend_far(head_rows, window)

    for distance in range(1, window):

        @pl.when(place == distance)
        def attend_inside():
            attend_far(rows, distance)

    def finish_soft(head, carry):
        span = lanes(head)
        soft_stage[:, span] = (acc[:, span] / total[head] * valid_col[...]).astype(jnp.bfloat16)
        return carry

    lax.fori_loop(0, heads, finish_soft, 0)
    soft_store = pltpu.make_async_copy(soft_stage, soft_hbm, out_sem.at[0])
    soft_store.start()

    loads[6].wait()
    for step in range(1, head_size):
        square_copy(step).wait_recv()
    summed = square_mine[...]
    for step in range(1, head_size):
        summed = summed + square_far[step - 1]
    inverse = lax.rsqrt(summed * (1.0 / (features * head_size)) + norm_eps)
    enter_all[...] = jnp.broadcast_to(inverse[0:1], (TILE, rows)).T * valid_col[...]

    def finish_lin(head, carry):
        span = lanes(head)
        opened = jax.nn.sigmoid(gate[:, span].astype(jnp.float32))
        lin_stage[:, span] = (lin[:, span] * enter_all[...] * gain_ref[:, span] * opened).astype(
            jnp.bfloat16
        )
        return carry

    lax.fori_loop(0, heads, finish_lin, 0)
    lin_store = pltpu.make_async_copy(lin_stage, lin_hbm, out_sem.at[1])
    lin_store.start()
    for distance in range(1, window + 1):

        @pl.when(sends(distance))
        def drain():
            for copy in far_copies(distance):
                copy.wait_send()

    for step in range(1, head_size):
        square_copy(step).wait_send()
    soft_store.wait()
    lin_store.wait()


def per_device(
    lin_query,
    lin_key,
    lin_value,
    lin_gate,
    lin_decay,
    norm_gain,
    soft_query,
    soft_key,
    soft_value,
    starts,
    lengths,
):
    rows, features = lin_query.shape
    kv_features = soft_key.shape[1]
    heads = features // TILE
    ctx_size, head_size = lax.axis_size("ctx"), lax.axis_size("head")
    window = ctx_size // starts.shape[0]
    f32, bf16 = jnp.float32, jnp.bfloat16
    anywhere = pl.BlockSpec(memory_space=pl.ANY)
    vmem = pl.BlockSpec(memory_space=pltpu.VMEM)
    smem = pl.BlockSpec(memory_space=pltpu.SMEM)
    wide = pltpu.VMEM((rows, features), bf16)
    narrow = pltpu.VMEM((rows, kv_features), bf16)
    dma = pltpu.SemaphoreType.DMA
    scratch = [wide, wide, wide, wide, wide, narrow, narrow]
    scratch += [
        pltpu.VMEM((window, rows, kv_features), bf16),
        pltpu.VMEM((window, rows, kv_features), bf16),
        pltpu.VMEM((heads, TILE, TILE), bf16),
        pltpu.VMEM((window, heads, TILE, TILE), bf16),
        pltpu.VMEM((heads, TILE), f32),
        pltpu.VMEM((window, heads, TILE), f32),
        pltpu.VMEM((rows, TILE), f32),
        pltpu.VMEM((TILE, rows), f32),
        pltpu.VMEM((rows, TILE), f32),
        pltpu.VMEM((rows, TILE), f32),
        pltpu.VMEM((rows, TILE), f32),
        pltpu.VMEM((rows, TILE), f32),
        pltpu.VMEM((window + 1, rows, rows), f32),
        pltpu.VMEM((rows, features), f32),
        pltpu.VMEM((heads, rows, TILE), f32),
        pltpu.VMEM((heads, rows, TILE), f32),
        pltpu.VMEM((rows, features), f32),
        pltpu.VMEM((8, rows), f32),
        pltpu.VMEM((head_size - 1, 8, rows), f32),
        wide,
        wide,
        dma((7,)),
        dma((2,)),
        dma((window, 2)),
        dma((window, 2)),
        dma((window, PARTS + 1)),
        dma((window, PARTS + 1)),
        dma((head_size - 1,)),
        dma((head_size - 1,)),
    ]
    out = jax.ShapeDtypeStruct((rows, features), bf16)
    return pl.pallas_call(
        functools.partial(kernel, ctx_size, head_size),
        out_shape=(out, out),
        in_specs=[anywhere] * 4 + [vmem, vmem] + [anywhere] * 3 + [smem, smem],
        out_specs=(anywhere, anywhere),
        scratch_shapes=scratch,
        compiler_params=pltpu.CompilerParams(
            collective_id=0, has_side_effects=True, vmem_limit_bytes=56 * 1024 * 1024
        ),
    )(
        lin_query,
        lin_key,
        lin_value,
        lin_gate,
        lin_decay,
        norm_gain.reshape(1, features),
        soft_query,
        soft_key,
        soft_value,
        starts,
        lengths,
    )


def solution(mesh):
    both = P("ctx", "head")
    placed = (both, both, both, both, both, P("head"), both, both, both, P(), P())
    return jax.shard_map(
        per_device, mesh=mesh, in_specs=placed, out_specs=(both, both), check_vma=False
    )
```

```python
import functools

import jax
import jax.numpy as jnp
from jax import lax
from jax.experimental import pallas as pl
from jax.experimental.pallas import tpu as pltpu
from jax.sharding import PartitionSpec as P

neg_big = -1e30
norm_eps = 1e-06
MESH = pl.DeviceIdType.MESH
TILE = 128
PARTS = 4
log2_e = 1.4426950408889634


def dot_rows(a, b):
    return lax.dot_general(a, b, (((1,), (1,)), ((), ())), preferred_element_type=jnp.float32)


def dot_plain(a, b):
    return jnp.dot(a, b, preferred_element_type=jnp.float32)


def kernel(
    ctx_size,
    head_size,
    lq_hbm,
    lk_hbm,
    lv_hbm,
    gate_hbm,
    decay_ref,
    gain_ref,
    sq_hbm,
    sk_hbm,
    sv_hbm,
    starts_ref,
    lengths_ref,
    lin_hbm,
    soft_hbm,
    lq,
    lk,
    lv,
    gate,
    sq,
    sk,
    sv,
    far_k,
    far_v,
    state_mine,
    state_far,
    total_mine,
    total_far,
    c_row,
    c_all,
    enter_all,
    end_all,
    valid_col,
    bias,
    lin,
    square_mine,
    square_far,
    lin_stage,
    soft_stage,
    in_sem,
    out_sem,
    kv_send,
    kv_recv,
    state_send,
    state_recv,
    square_send,
    square_recv,
):
    rows, features = lq.shape
    heads = features // TILE
    kv_count = sk.shape[1] // TILE
    group = heads // kv_count
    seqs = starts_ref.shape[0]
    window = ctx_size // seqs
    row_tiles = rows // TILE
    reach = min(window * rows // 8, rows // 2)
    head_rows = -(-reach // TILE) * TILE
    me = lax.axis_index("ctx")
    mine = lax.axis_index("head")
    place = lax.rem(me, window)
    first = me * rows
    opening = place == 0

    loads = [
        pltpu.make_async_copy(source, target, in_sem.at[i])
        for i, (source, target) in enumerate(
            ((lk_hbm, lk), (lv_hbm, lv), (lq_hbm, lq), (sk_hbm, sk), (sv_hbm, sv), (sq_hbm, sq), (gate_hbm, gate))
        )
    ]
    for load in loads:
        load.start()

    def receives(distance):
        return (opening & (me > 0)) | (place >= distance)

    def sends(distance):
        target = lax.rem(me + distance, window)
        return (me + distance < ctx_size) & ((target == 0) | (target >= distance))

    barrier = pltpu.get_barrier_semaphore()
    for distance in range(1, window + 1):

        @pl.when(receives(distance))
        def greet_source():
            pl.semaphore_signal(barrier, inc=1, device_id={"ctx": me - distance}, device_id_type=MESH)

        @pl.when(sends(distance))
        def greet_target():
            pl.semaphore_signal(barrier, inc=1, device_id={"ctx": me + distance}, device_id_type=MESH)

    for step in range(1, head_size):
        peer = lax.rem(mine + step, head_size)
        pl.semaphore_signal(barrier, inc=1, device_id={"head": peer}, device_id_type=MESH)

    def segment_of(pos):
        segment = jnp.full(pos.shape, -1, jnp.int32)
        for s in range(seqs):
            segment = segment + jnp.where(starts_ref[s] <= pos, 1, 0)
        stop = jnp.zeros(pos.shape, jnp.int32)
        for s in range(seqs):
            stop = jnp.where(segment == s, starts_ref[s] + lengths_ref[s], stop)
        return segment, (segment >= 0) & (pos < stop)

    def segment_at(pos):
        segment = jnp.int32(-1)
        for s in range(seqs):
            segment = segment + jnp.where(starts_ref[s] <= pos, 1, 0)
        return segment

    before = segment_at(first - 1)
    last = segment_at(first + rows - 1)
    row_pos = lax.broadcasted_iota(jnp.int32, (rows, TILE), 0) + first
    row_seg, row_valid = segment_of(row_pos)
    valid_col[...] = row_valid.astype(jnp.float32)

    def key_code(owner):
        pos = lax.broadcasted_iota(jnp.int32, (8, rows), 1) + owner * rows
        segment, valid = segment_of(pos)
        return jnp.where(valid, segment, -7)[0:1]

    query_seg = row_seg[:, 0:1]
    own_code = key_code(me)
    order = lax.broadcasted_iota(jnp.int32, (rows, rows), 1) <= lax.broadcasted_iota(
        jnp.int32, (rows, rows), 0
    )
    bias[0] = jnp.where(order & (query_seg == own_code), 0.0, neg_big)
    for distance in range(1, window + 1):
        bias[distance] = jnp.where(query_seg == key_code(me - distance), 0.0, neg_big)

    upper = jnp.where(
        lax.broadcasted_iota(jnp.int32, (rows, rows), 0)
        <= lax.broadcasted_iota(jnp.int32, (rows, rows), 1),
        log2_e,
        0.0,
    )
    c_row[...] = jnp.zeros_like(c_row)
    c_row[0:heads, :] = lax.dot_general(
        decay_ref[...],
        upper,
        (((1,), (0,)), ((), ())),
        precision=lax.Precision.HIGHEST,
        preferred_element_type=jnp.float32,
    )
    by_head = c_row[...]
    cumulative = by_head.T
    c_all[...] = cumulative
    enter_all[...] = jnp.where(row_seg == before, jnp.exp2(cumulative), 0.0)
    end_all[...] = jnp.where(
        (row_seg == last) & row_valid, jnp.exp2(cumulative[rows - 1 : rows] - cumulative), 0.0
    )
    whole = jnp.exp2(by_head[0:heads, rows - 1 : rows]) * jnp.where(last == before, 1.0, 0.0)
    total_mine[...] = jnp.broadcast_to(whole, (heads, TILE))

    greetings = head_size - 1
    for distance in range(1, window + 1):
        greetings = greetings + jnp.where(receives(distance), 1, 0)
        greetings = greetings + jnp.where(sends(distance), 1, 0)
    pl.semaphore_wait(barrier, greetings)

    def total_copy(distance):
        return pltpu.make_async_remote_copy(
            src_ref=total_mine,
            dst_ref=total_far.at[distance - 1],
            send_sem=state_send.at[distance - 1, PARTS],
            recv_sem=state_recv.at[distance - 1, PARTS],
            device_id={"ctx": me + distance},
            device_id_type=MESH,
        )

    share = heads // PARTS

    def state_copy(distance, part):
        span = pl.ds(part * share, share)
        return pltpu.make_async_remote_copy(
            src_ref=state_mine.at[span],
            dst_ref=state_far.at[distance - 1, span],
            send_sem=state_send.at[distance - 1, part],
            recv_sem=state_recv.at[distance - 1, part],
            device_id={"ctx": me + distance},
            device_id_type=MESH,
        )

    def kv_copies(distance):
        return [
            pltpu.make_async_remote_copy(
                src_ref=source,
                dst_ref=target.at[distance - 1],
                send_sem=kv_send.at[distance - 1, i],
                recv_sem=kv_recv.at[distance - 1, i],
                device_id={"ctx": me + distance},
                device_id_type=MESH,
            )
            for i, (source, target) in enumerate(((sk_hbm, far_k), (sv_hbm, far_v)))
        ]

    def far_copies(distance):
        return (
            [total_copy(distance)]
            + [state_copy(distance, part) for part in range(PARTS)]
            + kv_copies(distance)
        )

    def lanes(head):
        return pl.ds(pl.multiple_of(head * TILE, TILE), TILE)

    lane_id = lax.broadcasted_iota(jnp.int32, (rows, TILE), 1)

    def column(ref, head):
        return jnp.sum(jnp.where(lane_id == head, ref[...], 0.0), axis=1, keepdims=True)

    for distance in range(1, window + 1):

        @pl.when(sends(distance))
        def send_keys():
            for copy in kv_copies(distance):
                copy.start()

    loads[0].wait()
    loads[1].wait()

    def make_state(head):
        scaled = (lk[:, lanes(head)].astype(jnp.float32) * column(end_all, head)).astype(jnp.bfloat16)
        local = lax.dot_general(
            scaled, lv[:, lanes(head)], (((0,), (0,)), ((), ())), preferred_element_type=jnp.float32
        )
        return local.astype(jnp.bfloat16)

    for part in range(PARTS):
        made = [make_state(head) for head in range(part * share, (part + 1) * share)]
        for index, local in enumerate(made):
            state_mine[part * share + index] = local
        for distance in range(1, window + 1):

            @pl.when(sends(distance))
            def send_state():
                if part == 0:
                    total_copy(distance).start()
                state_copy(distance, part).start()

    loads[2].wait()

    def within(pair, carry):
        made = []
        for head in (2 * pair, 2 * pair + 1):
            c_col = column(c_all, head)
            c_line = c_row[pl.ds(head, 1), :]
            span = lanes(head)
            for tile in range(row_tiles):
                at = slice(tile * TILE, (tile + 1) * TILE)
                wide = (tile + 1) * TILE
                factor = jnp.exp2(c_col[at] - c_line[:, 0:wide] + bias[0, at, 0:wide])
                weights = (dot_rows(lq[at, span], lk[0:wide, span]) * factor).astype(jnp.bfloat16)
                made.append((at, span, dot_plain(weights, lv[0:wide, span])))
        for at, span, value in made:
            lin[at, span] = value
        return carry

    lax.fori_loop(0, heads // 2, within, 0)

    for load in loads[3:6]:
        load.wait()
    for distance in range(1, window + 1):

        @pl.when(receives(distance))
        def await_keys():
            for copy in kv_copies(distance):
                copy.wait_recv()

    score_scale = log2_e * TILE ** (-0.5)
    ones = jnp.ones((rows, TILE), jnp.bfloat16)

    def attend_all(pairs_from, pairs_to, far_rows, distances):
        def body(pair, carry):
            made = []
            for head in (2 * pair, 2 * pair + 1):
                span = lanes(head)
                kv_span = lanes(head // group)
                for tile in range(row_tiles):
                    at = slice(tile * TILE, (tile + 1) * TILE)
                    wide = (tile + 1) * TILE
                    query = sq[at, span]
                    pieces = [
                        (
                            dot_rows(query, sk[0:wide, kv_span]) * score_scale + bias[0, at, 0:wide],
                            sv[0:wide, kv_span],
                        )
                    ]
                    if tile * TILE < far_rows:
                        for index in range(distances):
                            scores = dot_rows(query, far_k[index, :, kv_span]) * score_scale
                            pieces.append((scores + bias[index + 1, at, :], far_v[index, :, kv_span]))
                    top = jnp.max(pieces[0][0], axis=1, keepdims=True)
                    for scores, value in pieces[1:]:
                        top = jnp.maximum(top, jnp.max(scores, axis=1, keepdims=True))
                    mixed = None
                    for scores, value in pieces:
                        probs = jnp.exp2(scores - top).astype(jnp.bfloat16)
                        both = jnp.concatenate([value, ones[0 : value.shape[0]]], axis=1)
                        term = dot_plain(probs, both)
                        mixed = term if mixed is None else mixed + term
                    result = mixed[:, 0:TILE] * (valid_col[at, :] / mixed[:, TILE:])
                    made.append((at, span, result.astype(jnp.bfloat16)))
            for at, span, value in made:
                soft_stage[at, span] = value
            return carry

        lax.fori_loop(pairs_from, pairs_to, body, 0)

    def attend(pairs_from, pairs_to):
        @pl.when(me == 0)
        def attend_own():
            attend_all(pairs_from, pairs_to, 0, 0)

        @pl.when(opening & (me > 0))
        def attend_opening():
            attend_all(pairs_from, pairs_to, head_rows, window)

        for distance in range(1, window):

            @pl.when(place == distance)
            def attend_inside():
                attend_all(pairs_from, pairs_to, rows, distance)

    attend(0, heads // 4)

    for distance in range(1, window + 1):

        @pl.when(receives(distance))
        def await_state():
            total_copy(distance).wait_recv()
            for part in range(PARTS):
                state_copy(distance, part).wait_recv()

    def carried_over(count, distances):
        def body(head, carry):
            state = state_far[0, head].astype(jnp.float32)
            if distances > 1:
                scale = total_far[0, pl.ds(head, 1), :]
                for index in range(1, distances):
                    state = state + scale * state_far[index, head].astype(jnp.float32)
                    scale = scale * total_far[index, pl.ds(head, 1), :]
            enter = column(enter_all, head)[0:count]
            span = lanes(head)
            lin[0:count, span] += enter * dot_plain(lq[0:count, span], state.astype(jnp.bfloat16))
            return carry

        lax.fori_loop(0, heads, body, 0)

    @pl.when(opening & (me > 0))
    def carry_opening():
        carried_over(head_rows, window)

    for distance in range(1, window):

        @pl.when(place == distance)
        def carry_inside():
            carried_over(rows, distance)

    def square(head, so_far):
        value = lin[:, lanes(head)] * valid_col[...]
        return so_far + value * value

    squares = lax.fori_loop(0, heads, square, jnp.zeros((rows, TILE), jnp.float32))
    square_mine[...] = lax.dot_general(
        jnp.ones((8, TILE), jnp.float32),
        squares,
        (((1,), (1,)), ((), ())),
        precision=lax.Precision.HIGHEST,
        preferred_element_type=jnp.float32,
    )

    def square_copy(step):
        return pltpu.make_async_remote_copy(
            src_ref=square_mine,
            dst_ref=square_far.at[step - 1],
            send_sem=square_send.at[step - 1],
            recv_sem=square_recv.at[step - 1],
            device_id={"head": lax.rem(mine + step, head_size)},
            device_id_type=MESH,
        )

    for step in range(1, head_size):
        square_copy(step).start()

    attend(heads // 4, heads // 2)
    soft_store = pltpu.make_async_copy(soft_stage, soft_hbm, out_sem.at[0])
    soft_store.start()

    loads[6].wait()
    for step in range(1, head_size):
        square_copy(step).wait_recv()
    summed = square_mine[...]
    for step in range(1, head_size):
        summed = summed + square_far[step - 1]
    inverse = lax.rsqrt(summed * (1.0 / (features * head_size)) + norm_eps)
    enter_all[...] = jnp.broadcast_to(inverse[0:1], (TILE, rows)).T * valid_col[...]

    def finish_lin(head, carry):
        span = lanes(head)
        opened = 0.5 + 0.5 * jnp.tanh(0.5 * gate[:, span].astype(jnp.float32))
        lin_stage[:, span] = (lin[:, span] * enter_all[...] * gain_ref[:, span] * opened).astype(
            jnp.bfloat16
        )
        return carry

    lax.fori_loop(0, heads, finish_lin, 0)
    lin_store = pltpu.make_async_copy(lin_stage, lin_hbm, out_sem.at[1])
    lin_store.start()
    for distance in range(1, window + 1):

        @pl.when(sends(distance))
        def drain():
            for copy in far_copies(distance):
                copy.wait_send()

    for step in range(1, head_size):
        square_copy(step).wait_send()
    soft_store.wait()
    lin_store.wait()


def per_device(
    lin_query,
    lin_key,
    lin_value,
    lin_gate,
    lin_decay,
    norm_gain,
    soft_query,
    soft_key,
    soft_value,
    starts,
    lengths,
):
    rows, features = lin_query.shape
    kv_features = soft_key.shape[1]
    heads = features // TILE
    ctx_size, head_size = lax.axis_size("ctx"), lax.axis_size("head")
    window = ctx_size // starts.shape[0]
    f32, bf16 = jnp.float32, jnp.bfloat16
    anywhere = pl.BlockSpec(memory_space=pl.ANY)
    vmem = pl.BlockSpec(memory_space=pltpu.VMEM)
    smem = pl.BlockSpec(memory_space=pltpu.SMEM)
    wide = pltpu.VMEM((rows, features), bf16)
    narrow = pltpu.VMEM((rows, kv_features), bf16)
    dma = pltpu.SemaphoreType.DMA
    scratch = [wide, wide, wide, wide, wide, narrow, narrow]
    scratch += [
        pltpu.VMEM((window, rows, kv_features), bf16),
        pltpu.VMEM((window, rows, kv_features), bf16),
        pltpu.VMEM((heads, TILE, TILE), bf16),
        pltpu.VMEM((window, heads, TILE, TILE), bf16),
        pltpu.VMEM((heads, TILE), f32),
        pltpu.VMEM((window, heads, TILE), f32),
        pltpu.VMEM((TILE, rows), f32),
        pltpu.VMEM((rows, TILE), f32),
        pltpu.VMEM((rows, TILE), f32),
        pltpu.VMEM((rows, TILE), f32),
        pltpu.VMEM((rows, TILE), f32),
        pltpu.VMEM((window + 1, rows, rows), f32),
        pltpu.VMEM((rows, features), f32),
        pltpu.VMEM((8, rows), f32),
        pltpu.VMEM((head_size - 1, 8, rows), f32),
        wide,
        wide,
        dma((7,)),
        dma((2,)),
        dma((window, 2)),
        dma((window, 2)),
        dma((window, PARTS + 1)),
        dma((window, PARTS + 1)),
        dma((head_size - 1,)),
        dma((head_size - 1,)),
    ]
    out = jax.ShapeDtypeStruct((rows, features), bf16)
    return pl.pallas_call(
        functools.partial(kernel, ctx_size, head_size),
        out_shape=(out, out),
        in_specs=[anywhere] * 4 + [vmem, vmem] + [anywhere] * 3 + [smem, smem],
        out_specs=(anywhere, anywhere),
        scratch_shapes=scratch,
        compiler_params=pltpu.CompilerParams(
            collective_id=0, has_side_effects=True, vmem_limit_bytes=56 * 1024 * 1024
        ),
    )(
        lin_query,
        lin_key,
        lin_value,
        lin_gate,
        lin_decay.T,
        norm_gain.reshape(1, features),
        soft_query,
        soft_key,
        soft_value,
        starts,
        lengths,
    )


def solution(mesh):
    both = P("ctx", "head")
    placed = (both, both, both, both, both, P("head"), both, both, both, P(), P())
    return jax.shard_map(
        per_device, mesh=mesh, in_specs=placed, out_specs=(both, both), check_vma=False
    )
```

```python
import functools

import jax
import jax.numpy as jnp
from jax import lax
from jax.experimental import pallas as pl
from jax.experimental.pallas import tpu as pltpu
from jax.sharding import PartitionSpec as P

neg_big = -1e30
norm_eps = 1e-06
MESH = pl.DeviceIdType.MESH
TILE = 128
PARTS = 4
log2_e = 1.4426950408889634


def dot_rows(a, b):
    return lax.dot_general(a, b, (((1,), (1,)), ((), ())), preferred_element_type=jnp.float32)


def dot_plain(a, b):
    return jnp.dot(a, b, preferred_element_type=jnp.float32)


def kernel(
    ctx_size,
    head_size,
    lq_hbm,
    lk_hbm,
    lv_hbm,
    gate_hbm,
    decay_ref,
    gain_ref,
    sq_hbm,
    sk_hbm,
    sv_hbm,
    starts_ref,
    lengths_ref,
    lin_hbm,
    soft_hbm,
    lq,
    lk,
    lv,
    gate,
    sq,
    sk,
    sv,
    far_k,
    far_v,
    state_mine,
    state_far,
    total_mine,
    total_far,
    c_row,
    c_all,
    enter_all,
    end_all,
    valid_col,
    bias,
    lin,
    square_mine,
    square_far,
    lin_stage,
    soft_stage,
    in_sem,
    out_sem,
    kv_send,
    kv_recv,
    state_send,
    state_recv,
    square_send,
    square_recv,
):
    rows, features = lq.shape
    heads = features // TILE
    kv_count = sk.shape[1] // TILE
    group = heads // kv_count
    seqs = starts_ref.shape[0]
    window = ctx_size // seqs
    row_tiles = rows // TILE
    reach = min(window * rows // 8, rows // 2)
    head_rows = -(-reach // TILE) * TILE
    me = lax.axis_index("ctx")
    mine = lax.axis_index("head")
    place = lax.rem(me, window)
    first = me * rows
    opening = place == 0

    loads = [
        pltpu.make_async_copy(source, target, in_sem.at[i])
        for i, (source, target) in enumerate(
            ((lk_hbm, lk), (lv_hbm, lv), (lq_hbm, lq), (sk_hbm, sk), (sv_hbm, sv), (sq_hbm, sq), (gate_hbm, gate))
        )
    ]
    for load in loads:
        load.start()

    def receives(distance):
        return (opening & (me > 0)) | (place >= distance)

    def sends(distance):
        target = lax.rem(me + distance, window)
        return (me + distance < ctx_size) & ((target == 0) | (target >= distance))

    barrier = pltpu.get_barrier_semaphore()
    for distance in range(1, window + 1):

        @pl.when(receives(distance))
        def greet_source():
            pl.semaphore_signal(barrier, inc=1, device_id={"ctx": me - distance}, device_id_type=MESH)

        @pl.when(sends(distance))
        def greet_target():
            pl.semaphore_signal(barrier, inc=1, device_id={"ctx": me + distance}, device_id_type=MESH)

    for step in range(1, head_size):
        peer = lax.rem(mine + step, head_size)
        pl.semaphore_signal(barrier, inc=1, device_id={"head": peer}, device_id_type=MESH)

    def segment_of(pos):
        segment = jnp.full(pos.shape, -1, jnp.int32)
        for s in range(seqs):
            segment = segment + jnp.where(starts_ref[s] <= pos, 1, 0)
        stop = jnp.zeros(pos.shape, jnp.int32)
        for s in range(seqs):
            stop = jnp.where(segment == s, starts_ref[s] + lengths_ref[s], stop)
        return segment, (segment >= 0) & (pos < stop)

    def segment_at(pos):
        segment = jnp.int32(-1)
        for s in range(seqs):
            segment = segment + jnp.where(starts_ref[s] <= pos, 1, 0)
        return segment

    before = segment_at(first - 1)
    last = segment_at(first + rows - 1)
    row_pos = lax.broadcasted_iota(jnp.int32, (rows, TILE), 0) + first
    row_seg, row_valid = segment_of(row_pos)
    valid_col[...] = row_valid.astype(jnp.float32)

    def key_code(owner):
        pos = lax.broadcasted_iota(jnp.int32, (8, rows), 1) + owner * rows
        segment, valid = segment_of(pos)
        return jnp.where(valid, segment, -7)[0:1]

    query_seg = row_seg[:, 0:1]
    own_code = key_code(me)
    order = lax.broadcasted_iota(jnp.int32, (rows, rows), 1) <= lax.broadcasted_iota(
        jnp.int32, (rows, rows), 0
    )
    bias[0] = jnp.where(order & (query_seg == own_code), 0.0, neg_big)
    for distance in range(1, window + 1):
        bias[distance] = jnp.where(query_seg == key_code(me - distance), 0.0, neg_big)

    upper = jnp.where(
        lax.broadcasted_iota(jnp.int32, (rows, rows), 0)
        <= lax.broadcasted_iota(jnp.int32, (rows, rows), 1),
        log2_e,
        0.0,
    )
    c_row[...] = jnp.zeros_like(c_row)
    c_row[0:heads, :] = lax.dot_general(
        decay_ref[...],
        upper,
        (((1,), (0,)), ((), ())),
        precision=lax.Precision.HIGHEST,
        preferred_element_type=jnp.float32,
    )
    by_head = c_row[...]
    cumulative = by_head.T
    c_all[...] = cumulative
    enter_all[...] = jnp.where(row_seg == before, jnp.exp2(cumulative), 0.0)
    end_all[...] = jnp.where(
        (row_seg == last) & row_valid, jnp.exp2(cumulative[rows - 1 : rows] - cumulative), 0.0
    )
    whole = jnp.exp2(by_head[0:heads, rows - 1 : rows]) * jnp.where(last == before, 1.0, 0.0)
    total_mine[...] = jnp.broadcast_to(whole, (heads, TILE))

    greetings = head_size - 1
    for distance in range(1, window + 1):
        greetings = greetings + jnp.where(receives(distance), 1, 0)
        greetings = greetings + jnp.where(sends(distance), 1, 0)
    pl.semaphore_wait(barrier, greetings)

    def total_copy(distance):
        return pltpu.make_async_remote_copy(
            src_ref=total_mine,
            dst_ref=total_far.at[distance - 1],
            send_sem=state_send.at[distance - 1, PARTS],
            recv_sem=state_recv.at[distance - 1, PARTS],
            device_id={"ctx": me + distance},
            device_id_type=MESH,
        )

    share = heads // PARTS

    def state_copy(distance, part):
        span = pl.ds(part * share, share)
        return pltpu.make_async_remote_copy(
            src_ref=state_mine.at[span],
            dst_ref=state_far.at[distance - 1, span],
            send_sem=state_send.at[distance - 1, part],
            recv_sem=state_recv.at[distance - 1, part],
            device_id={"ctx": me + distance},
            device_id_type=MESH,
        )

    def kv_copies(distance):
        return [
            pltpu.make_async_remote_copy(
                src_ref=source,
                dst_ref=target.at[distance - 1],
                send_sem=kv_send.at[distance - 1, i],
                recv_sem=kv_recv.at[distance - 1, i],
                device_id={"ctx": me + distance},
                device_id_type=MESH,
            )
            for i, (source, target) in enumerate(((sk_hbm, far_k), (sv_hbm, far_v)))
        ]

    def far_copies(distance):
        return (
            [total_copy(distance)]
            + [state_copy(distance, part) for part in range(PARTS)]
            + kv_copies(distance)
        )

    def lanes(head):
        return pl.ds(pl.multiple_of(head * TILE, TILE), TILE)

    lane_id = lax.broadcasted_iota(jnp.int32, (rows, TILE), 1)

    def column(ref, head):
        return jnp.sum(jnp.where(lane_id == head, ref[...], 0.0), axis=1, keepdims=True)

    for distance in range(1, window + 1):

        @pl.when(sends(distance))
        def send_keys():
            for copy in kv_copies(distance):
                copy.start()

    loads[0].wait()
    loads[1].wait()

    def make_state(head):
        scaled = (lk[:, lanes(head)].astype(jnp.float32) * column(end_all, head)).astype(jnp.bfloat16)
        local = lax.dot_general(
            scaled, lv[:, lanes(head)], (((0,), (0,)), ((), ())), preferred_element_type=jnp.float32
        )
        return local.astype(jnp.bfloat16)

    for part in range(PARTS):
        made = [make_state(head) for head in range(part * share, (part + 1) * share)]
        for index, local in enumerate(made):
            state_mine[part * share + index] = local
        for distance in range(1, window + 1):

            @pl.when(sends(distance))
            def send_state():
                if part == 0:
                    total_copy(distance).start()
                state_copy(distance, part).start()

    loads[2].wait()

    def within(quad, carry):
        made = []
        for head in [4 * quad + i for i in range(4)]:
            c_col = column(c_all, head)
            c_line = c_row[pl.ds(head, 1), :]
            span = lanes(head)
            for tile in range(row_tiles):
                at = slice(tile * TILE, (tile + 1) * TILE)
                wide = (tile + 1) * TILE
                factor = jnp.exp2(c_col[at] - c_line[:, 0:wide] + bias[0, at, 0:wide])
                weights = (dot_rows(lq[at, span], lk[0:wide, span]) * factor).astype(jnp.bfloat16)
                made.append((at, span, dot_plain(weights, lv[0:wide, span])))
        for at, span, value in made:
            lin[at, span] = value
        return carry

    lax.fori_loop(0, heads // 4, within, 0)

    for load in loads[3:6]:
        load.wait()
    for distance in range(1, window + 1):

        @pl.when(receives(distance))
        def await_keys():
            for copy in kv_copies(distance):
                copy.wait_recv()

    score_scale = log2_e * TILE ** (-0.5)
    ones = jnp.ones((rows, TILE), jnp.bfloat16)

    def attend_all(pairs_from, pairs_to, far_rows, distances):
        def body(pair, carry):
            made = []
            for head in (2 * pair, 2 * pair + 1):
                span = lanes(head)
                kv_span = lanes(head // group)
                for tile in range(row_tiles):
                    at = slice(tile * TILE, (tile + 1) * TILE)
                    wide = (tile + 1) * TILE
                    query = sq[at, span]
                    pieces = [
                        (
                            dot_rows(query, sk[0:wide, kv_span]) * score_scale + bias[0, at, 0:wide],
                            sv[0:wide, kv_span],
                        )
                    ]
                    if tile * TILE < far_rows:
                        for index in range(distances):
                            scores = dot_rows(query, far_k[index, :, kv_span]) * score_scale
                            pieces.append((scores + bias[index + 1, at, :], far_v[index, :, kv_span]))
                    top = jnp.max(pieces[0][0], axis=1, keepdims=True)
                    for scores, value in pieces[1:]:
                        top = jnp.maximum(top, jnp.max(scores, axis=1, keepdims=True))
                    mixed = None
                    for scores, value in pieces:
                        probs = jnp.exp2(scores - top).astype(jnp.bfloat16)
                        both = jnp.concatenate([value, ones[0 : value.shape[0]]], axis=1)
                        term = dot_plain(probs, both)
                        mixed = term if mixed is None else mixed + term
                    result = mixed[:, 0:TILE] * (valid_col[at, :] / mixed[:, TILE:])
                    made.append((at, span, result.astype(jnp.bfloat16)))
            for at, span, value in made:
                soft_stage[at, span] = value
            return carry

        lax.fori_loop(pairs_from, pairs_to, body, 0)

    def attend(pairs_from, pairs_to):
        @pl.when(me == 0)
        def attend_own():
            attend_all(pairs_from, pairs_to, 0, 0)

        @pl.when(opening & (me > 0))
        def attend_opening():
            attend_all(pairs_from, pairs_to, head_rows, window)

        for distance in range(1, window):

            @pl.when(place == distance)
            def attend_inside():
                attend_all(pairs_from, pairs_to, rows, distance)

    attend(0, heads // 4)

    for distance in range(1, window + 1):

        @pl.when(receives(distance))
        def await_state():
            total_copy(distance).wait_recv()
            for part in range(PARTS):
                state_copy(distance, part).wait_recv()

    def carried_over(count, distances):
        def body(quad, carry):
            made = []
            for head in [4 * quad + i for i in range(4)]:
                state = state_far[0, head]
                if distances > 1:
                    state = state.astype(jnp.float32)
                    scale = total_far[0, pl.ds(head, 1), :]
                    for index in range(1, distances):
                        state = state + scale * state_far[index, head].astype(jnp.float32)
                        scale = scale * total_far[index, pl.ds(head, 1), :]
                    state = state.astype(jnp.bfloat16)
                enter = column(enter_all, head)[0:count]
                span = lanes(head)
                made.append((span, lin[0:count, span] + enter * dot_plain(lq[0:count, span], state)))
            for span, value in made:
                lin[0:count, span] = value
            return carry

        lax.fori_loop(0, heads // 4, body, 0)

    @pl.when(opening & (me > 0))
    def carry_opening():
        carried_over(head_rows, window)

    for distance in range(1, window):

        @pl.when(place == distance)
        def carry_inside():
            carried_over(rows, distance)

    def square(quad, so_far):
        for head in [4 * quad + i for i in range(4)]:
            value = lin[:, lanes(head)]
            so_far = so_far + value * value
        return so_far

    squares = lax.fori_loop(0, heads // 4, square, jnp.zeros((rows, TILE), jnp.float32))
    squares = squares * valid_col[...]
    square_mine[...] = lax.dot_general(
        jnp.ones((8, TILE), jnp.float32),
        squares,
        (((1,), (1,)), ((), ())),
        precision=lax.Precision.HIGHEST,
        preferred_element_type=jnp.float32,
    )

    def square_copy(step):
        return pltpu.make_async_remote_copy(
            src_ref=square_mine,
            dst_ref=square_far.at[step - 1],
            send_sem=square_send.at[step - 1],
            recv_sem=square_recv.at[step - 1],
            device_id={"head": lax.rem(mine + step, head_size)},
            device_id_type=MESH,
        )

    for step in range(1, head_size):
        square_copy(step).start()

    attend(heads // 4, heads // 2)
    soft_store = pltpu.make_async_copy(soft_stage, soft_hbm, out_sem.at[0])
    soft_store.start()

    loads[6].wait()
    for step in range(1, head_size):
        square_copy(step).wait_recv()
    summed = square_mine[...]
    for step in range(1, head_size):
        summed = summed + square_far[step - 1]
    inverse = lax.rsqrt(summed * (1.0 / (features * head_size)) + norm_eps)
    enter_all[...] = jnp.broadcast_to(inverse[0:1], (TILE, rows)).T * valid_col[...]

    def finish_lin(quad, carry):
        made = []
        for head in [4 * quad + i for i in range(4)]:
            span = lanes(head)
            opened = 0.5 + 0.5 * jnp.tanh(0.5 * gate[:, span].astype(jnp.float32))
            value = lin[:, span] * enter_all[...] * gain_ref[:, span] * opened
            made.append((span, value.astype(jnp.bfloat16)))
        for span, value in made:
            lin_stage[:, span] = value
        return carry

    lax.fori_loop(0, heads // 4, finish_lin, 0)
    lin_store = pltpu.make_async_copy(lin_stage, lin_hbm, out_sem.at[1])
    lin_store.start()
    for distance in range(1, window + 1):

        @pl.when(sends(distance))
        def drain():
            for copy in far_copies(distance):
                copy.wait_send()

    for step in range(1, head_size):
        square_copy(step).wait_send()
    soft_store.wait()
    lin_store.wait()


def per_device(
    lin_query,
    lin_key,
    lin_value,
    lin_gate,
    lin_decay,
    norm_gain,
    soft_query,
    soft_key,
    soft_value,
    starts,
    lengths,
):
    rows, features = lin_query.shape
    kv_features = soft_key.shape[1]
    heads = features // TILE
    ctx_size, head_size = lax.axis_size("ctx"), lax.axis_size("head")
    window = ctx_size // starts.shape[0]
    f32, bf16 = jnp.float32, jnp.bfloat16
    anywhere = pl.BlockSpec(memory_space=pl.ANY)
    vmem = pl.BlockSpec(memory_space=pltpu.VMEM)
    smem = pl.BlockSpec(memory_space=pltpu.SMEM)
    wide = pltpu.VMEM((rows, features), bf16)
    narrow = pltpu.VMEM((rows, kv_features), bf16)
    dma = pltpu.SemaphoreType.DMA
    scratch = [wide, wide, wide, wide, wide, narrow, narrow]
    scratch += [
        pltpu.VMEM((window, rows, kv_features), bf16),
        pltpu.VMEM((window, rows, kv_features), bf16),
        pltpu.VMEM((heads, TILE, TILE), bf16),
        pltpu.VMEM((window, heads, TILE, TILE), bf16),
        pltpu.VMEM((heads, TILE), f32),
        pltpu.VMEM((window, heads, TILE), f32),
        pltpu.VMEM((TILE, rows), f32),
        pltpu.VMEM((rows, TILE), f32),
        pltpu.VMEM((rows, TILE), f32),
        pltpu.VMEM((rows, TILE), f32),
        pltpu.VMEM((rows, TILE), f32),
        pltpu.VMEM((window + 1, rows, rows), f32),
        pltpu.VMEM((rows, features), f32),
        pltpu.VMEM((8, rows), f32),
        pltpu.VMEM((head_size - 1, 8, rows), f32),
        wide,
        wide,
        dma((7,)),
        dma((2,)),
        dma((window, 2)),
        dma((window, 2)),
        dma((window, PARTS + 1)),
        dma((window, PARTS + 1)),
        dma((head_size - 1,)),
        dma((head_size - 1,)),
    ]
    out = jax.ShapeDtypeStruct((rows, features), bf16)
    return pl.pallas_call(
        functools.partial(kernel, ctx_size, head_size),
        out_shape=(out, out),
        in_specs=[anywhere] * 4 + [vmem, vmem] + [anywhere] * 3 + [smem, smem],
        out_specs=(anywhere, anywhere),
        scratch_shapes=scratch,
        compiler_params=pltpu.CompilerParams(
            collective_id=0, has_side_effects=True, vmem_limit_bytes=56 * 1024 * 1024
        ),
    )(
        lin_query,
        lin_key,
        lin_value,
        lin_gate,
        lin_decay.T,
        norm_gain.reshape(1, features),
        soft_query,
        soft_key,
        soft_value,
        starts,
        lengths,
    )


def solution(mesh):
    both = P("ctx", "head")
    placed = (both, both, both, both, both, P("head"), both, both, both, P(), P())
    return jax.shard_map(
        per_device, mesh=mesh, in_specs=placed, out_specs=(both, both), check_vma=False
    )
```

```python
import functools

import jax
import jax.numpy as jnp
from jax import lax
from jax.experimental import pallas as pl
from jax.experimental.pallas import tpu as pltpu
from jax.sharding import PartitionSpec as P

neg_big = -1e30
norm_eps = 1e-06
MESH = pl.DeviceIdType.MESH
TILE = 128
PARTS = 4
log2_e = 1.4426950408889634


def dot_rows(a, b):
    return lax.dot_general(a, b, (((1,), (1,)), ((), ())), preferred_element_type=jnp.float32)


def dot_plain(a, b):
    return jnp.dot(a, b, preferred_element_type=jnp.float32)


def kernel(
    ctx_size,
    head_size,
    lq_hbm,
    lk_hbm,
    lv_hbm,
    gate_hbm,
    decay_ref,
    gain_ref,
    sq_hbm,
    sk_hbm,
    sv_hbm,
    starts_ref,
    lengths_ref,
    lin_hbm,
    soft_hbm,
    lq,
    lk,
    lv,
    gate,
    sq,
    sk,
    sv,
    far_k,
    far_v,
    state_mine,
    state_far,
    total_mine,
    total_far,
    c_row,
    c_all,
    enter_all,
    end_all,
    valid_col,
    bias,
    lin,
    square_mine,
    square_far,
    lin_stage,
    soft_stage,
    in_sem,
    out_sem,
    kv_send,
    kv_recv,
    state_send,
    state_recv,
    square_send,
    square_recv,
):
    rows, features = lq.shape
    heads = features // TILE
    kv_count = sk.shape[1] // TILE
    group = heads // kv_count
    seqs = starts_ref.shape[0]
    window = ctx_size // seqs
    row_tiles = rows // TILE
    reach = min(window * rows // 8, rows // 2)
    head_rows = -(-reach // TILE) * TILE
    me = lax.axis_index("ctx")
    mine = lax.axis_index("head")
    place = lax.rem(me, window)
    first = me * rows
    opening = place == 0

    loads = [
        pltpu.make_async_copy(source, target, in_sem.at[i])
        for i, (source, target) in enumerate(
            ((lk_hbm, lk), (lv_hbm, lv), (lq_hbm, lq), (sk_hbm, sk), (sv_hbm, sv), (sq_hbm, sq), (gate_hbm, gate))
        )
    ]
    for load in loads:
        load.start()

    def receives(distance):
        return (opening & (me > 0)) | (place >= distance)

    def sends(distance):
        target = lax.rem(me + distance, window)
        return (me + distance < ctx_size) & ((target == 0) | (target >= distance))

    barrier = pltpu.get_barrier_semaphore()
    for distance in range(1, window + 1):

        @pl.when(receives(distance))
        def greet_source():
            pl.semaphore_signal(barrier, inc=1, device_id={"ctx": me - distance}, device_id_type=MESH)

        @pl.when(sends(distance))
        def greet_target():
            pl.semaphore_signal(barrier, inc=1, device_id={"ctx": me + distance}, device_id_type=MESH)

    for step in range(1, head_size):
        peer = lax.rem(mine + step, head_size)
        pl.semaphore_signal(barrier, inc=1, device_id={"head": peer}, device_id_type=MESH)

    def segment_of(pos):
        segment = jnp.full(pos.shape, -1, jnp.int32)
        for s in range(seqs):
            segment = segment + jnp.where(starts_ref[s] <= pos, 1, 0)
        stop = jnp.zeros(pos.shape, jnp.int32)
        for s in range(seqs):
            stop = jnp.where(segment == s, starts_ref[s] + lengths_ref[s], stop)
        return segment, (segment >= 0) & (pos < stop)

    def segment_at(pos):
        segment = jnp.int32(-1)
        for s in range(seqs):
            segment = segment + jnp.where(starts_ref[s] <= pos, 1, 0)
        return segment

    before = segment_at(first - 1)
    last = segment_at(first + rows - 1)
    row_pos = lax.broadcasted_iota(jnp.int32, (rows, TILE), 0) + first
    row_seg, row_valid = segment_of(row_pos)
    valid_col[...] = row_valid.astype(jnp.float32)

    def key_code(owner):
        pos = lax.broadcasted_iota(jnp.int32, (8, rows), 1) + owner * rows
        segment, valid = segment_of(pos)
        return jnp.where(valid, segment, -7)[0:1]

    query_seg = row_seg[:, 0:1]
    own_code = key_code(me)
    order = lax.broadcasted_iota(jnp.int32, (rows, rows), 1) <= lax.broadcasted_iota(
        jnp.int32, (rows, rows), 0
    )
    bias[0] = jnp.where(order & (query_seg == own_code), 0.0, neg_big)
    for distance in range(1, window + 1):
        bias[distance] = jnp.where(query_seg == key_code(me - distance), 0.0, neg_big)

    upper = jnp.where(
        lax.broadcasted_iota(jnp.int32, (rows, rows), 0)
        <= lax.broadcasted_iota(jnp.int32, (rows, rows), 1),
        log2_e,
        0.0,
    )
    c_row[...] = jnp.zeros_like(c_row)
    c_row[0:heads, :] = lax.dot_general(
        decay_ref[...],
        upper,
        (((1,), (0,)), ((), ())),
        precision=lax.Precision.HIGHEST,
        preferred_element_type=jnp.float32,
    )
    by_head = c_row[...]
    cumulative = by_head.T
    c_all[...] = cumulative
    enter_all[...] = jnp.where(row_seg == before, jnp.exp2(cumulative), 0.0)
    end_all[...] = jnp.where(
        (row_seg == last) & row_valid, jnp.exp2(cumulative[rows - 1 : rows] - cumulative), 0.0
    )
    whole = jnp.exp2(by_head[0:heads, rows - 1 : rows]) * jnp.where(last == before, 1.0, 0.0)
    total_mine[...] = jnp.broadcast_to(whole, (heads, TILE))

    greetings = head_size - 1
    for distance in range(1, window + 1):
        greetings = greetings + jnp.where(receives(distance), 1, 0)
        greetings = greetings + jnp.where(sends(distance), 1, 0)
    pl.semaphore_wait(barrier, greetings)

    def total_copy(distance):
        return pltpu.make_async_remote_copy(
            src_ref=total_mine,
            dst_ref=total_far.at[distance - 1],
            send_sem=state_send.at[distance - 1, PARTS],
            recv_sem=state_recv.at[distance - 1, PARTS],
            device_id={"ctx": me + distance},
            device_id_type=MESH,
        )

    share = heads // PARTS

    def state_copy(distance, part):
        span = pl.ds(part * share, share)
        return pltpu.make_async_remote_copy(
            src_ref=state_mine.at[span],
            dst_ref=state_far.at[distance - 1, span],
            send_sem=state_send.at[distance - 1, part],
            recv_sem=state_recv.at[distance - 1, part],
            device_id={"ctx": me + distance},
            device_id_type=MESH,
        )

    def kv_copies(distance):
        return [
            pltpu.make_async_remote_copy(
                src_ref=source,
                dst_ref=target.at[distance - 1],
                send_sem=kv_send.at[distance - 1, i],
                recv_sem=kv_recv.at[distance - 1, i],
                device_id={"ctx": me + distance},
                device_id_type=MESH,
            )
            for i, (source, target) in enumerate(((sk_hbm, far_k), (sv_hbm, far_v)))
        ]

    def far_copies(distance):
        return (
            [total_copy(distance)]
            + [state_copy(distance, part) for part in range(PARTS)]
            + kv_copies(distance)
        )

    def lanes(head):
        return pl.ds(pl.multiple_of(head * TILE, TILE), TILE)

    lane_id = lax.broadcasted_iota(jnp.int32, (rows, TILE), 1)

    def column(ref, head):
        return jnp.sum(jnp.where(lane_id == head, ref[...], 0.0), axis=1, keepdims=True)

    for distance in range(1, window + 1):

        @pl.when(sends(distance))
        def send_keys():
            for copy in kv_copies(distance):
                copy.start()

    loads[0].wait()
    loads[1].wait()

    def make_state(head):
        scaled = (lk[:, lanes(head)].astype(jnp.float32) * column(end_all, head)).astype(jnp.bfloat16)
        local = lax.dot_general(
            scaled, lv[:, lanes(head)], (((0,), (0,)), ((), ())), preferred_element_type=jnp.float32
        )
        return local.astype(jnp.bfloat16)

    for part in range(PARTS):
        made = [make_state(head) for head in range(part * share, (part + 1) * share)]
        for index, local in enumerate(made):
            state_mine[part * share + index] = local
        for distance in range(1, window + 1):

            @pl.when(sends(distance))
            def send_state():
                if part == 0:
                    total_copy(distance).start()
                state_copy(distance, part).start()

    loads[2].wait()

    def within(quad, carry):
        made = []
        for head in [4 * quad + i for i in range(4)]:
            c_col = column(c_all, head)
            c_line = c_row[pl.ds(head, 1), :]
            span = lanes(head)
            for tile in range(row_tiles):
                at = slice(tile * TILE, (tile + 1) * TILE)
                wide = (tile + 1) * TILE
                factor = jnp.exp2(c_col[at] - c_line[:, 0:wide] + bias[0, at, 0:wide])
                weights = (dot_rows(lq[at, span], lk[0:wide, span]) * factor).astype(jnp.bfloat16)
                made.append((at, span, dot_plain(weights, lv[0:wide, span])))
        for at, span, value in made:
            lin[at, span] = value
        return carry

    lax.fori_loop(0, heads // 4, within, 0)

    for load in loads[3:6]:
        load.wait()
    for distance in range(1, window + 1):

        @pl.when(receives(distance))
        def await_keys():
            for copy in kv_copies(distance):
                copy.wait_recv()

    score_scale = log2_e * TILE ** (-0.5)
    ones = jnp.ones((rows, TILE), jnp.bfloat16)

    def attend_all(pairs_from, pairs_to, far_rows, distances):
        def body(pair, carry):
            made = []
            for head in (2 * pair, 2 * pair + 1):
                span = lanes(head)
                kv_span = lanes(head // group)
                for tile in range(row_tiles):
                    at = slice(tile * TILE, (tile + 1) * TILE)
                    wide = (tile + 1) * TILE
                    query = sq[at, span]
                    pieces = [
                        (
                            dot_rows(query, sk[0:wide, kv_span]) * score_scale + bias[0, at, 0:wide],
                            sv[0:wide, kv_span],
                        )
                    ]
                    if tile * TILE < far_rows:
                        for index in range(distances):
                            scores = dot_rows(query, far_k[index, :, kv_span]) * score_scale
                            pieces.append((scores + bias[index + 1, at, :], far_v[index, :, kv_span]))
                    top = jnp.max(pieces[0][0], axis=1, keepdims=True)
                    for scores, value in pieces[1:]:
                        top = jnp.maximum(top, jnp.max(scores, axis=1, keepdims=True))
                    mixed = None
                    for scores, value in pieces:
                        probs = jnp.exp2(scores - top).astype(jnp.bfloat16)
                        both = jnp.concatenate([value, ones[0 : value.shape[0]]], axis=1)
                        term = dot_plain(probs, both)
                        mixed = term if mixed is None else mixed + term
                    result = mixed[:, 0:TILE] * (valid_col[at, :] / mixed[:, TILE:])
                    made.append((at, span, result.astype(jnp.bfloat16)))
            for at, span, value in made:
                soft_stage[at, span] = value
            return carry

        lax.fori_loop(pairs_from, pairs_to, body, 0)

    def attend(pairs_from, pairs_to):
        @pl.when(me == 0)
        def attend_own():
            attend_all(pairs_from, pairs_to, 0, 0)

        @pl.when(opening & (me > 0))
        def attend_opening():
            attend_all(pairs_from, pairs_to, head_rows, window)

        for distance in range(1, window):

            @pl.when(place == distance)
            def attend_inside():
                attend_all(pairs_from, pairs_to, rows, distance)

    attend(0, 3 * heads // 8)

    for distance in range(1, window + 1):

        @pl.when(receives(distance))
        def await_state():
            total_copy(distance).wait_recv()
            for part in range(PARTS):
                state_copy(distance, part).wait_recv()

    def carried_over(count, distances):
        def body(quad, carry):
            made = []
            for head in [4 * quad + i for i in range(4)]:
                state = state_far[0, head]
                if distances > 1:
                    state = state.astype(jnp.float32)
                    scale = total_far[0, pl.ds(head, 1), :]
                    for index in range(1, distances):
                        state = state + scale * state_far[index, head].astype(jnp.float32)
                        scale = scale * total_far[index, pl.ds(head, 1), :]
                    state = state.astype(jnp.bfloat16)
                enter = column(enter_all, head)[0:count]
                span = lanes(head)
                made.append((span, lin[0:count, span] + enter * dot_plain(lq[0:count, span], state)))
            for span, value in made:
                lin[0:count, span] = value
            return carry

        lax.fori_loop(0, heads // 4, body, 0)

    @pl.when(opening & (me > 0))
    def carry_opening():
        carried_over(head_rows, window)

    for distance in range(1, window):

        @pl.when(place == distance)
        def carry_inside():
            carried_over(rows, distance)

    def square(quad, so_far):
        for head in [4 * quad + i for i in range(4)]:
            value = lin[:, lanes(head)]
            so_far = so_far + value * value
        return so_far

    squares = lax.fori_loop(0, heads // 4, square, jnp.zeros((rows, TILE), jnp.float32))
    squares = squares * valid_col[...]
    square_mine[...] = lax.dot_general(
        jnp.ones((8, TILE), jnp.float32),
        squares,
        (((1,), (1,)), ((), ())),
        precision=lax.Precision.HIGHEST,
        preferred_element_type=jnp.float32,
    )

    def square_copy(step):
        return pltpu.make_async_remote_copy(
            src_ref=square_mine,
            dst_ref=square_far.at[step - 1],
            send_sem=square_send.at[step - 1],
            recv_sem=square_recv.at[step - 1],
            device_id={"head": lax.rem(mine + step, head_size)},
            device_id_type=MESH,
        )

    for step in range(1, head_size):
        square_copy(step).start()

    attend(3 * heads // 8, heads // 2)
    soft_store = pltpu.make_async_copy(soft_stage, soft_hbm, out_sem.at[0])
    soft_store.start()

    loads[6].wait()
    for step in range(1, head_size):
        square_copy(step).wait_recv()
    summed = square_mine[...]
    for step in range(1, head_size):
        summed = summed + square_far[step - 1]
    inverse = lax.rsqrt(summed * (1.0 / (features * head_size)) + norm_eps)
    enter_all[...] = jnp.broadcast_to(inverse[0:1], (TILE, rows)).T * valid_col[...]

    def finish_lin(quad, carry):
        made = []
        for head in [4 * quad + i for i in range(4)]:
            span = lanes(head)
            opened = 0.5 + 0.5 * jnp.tanh(0.5 * gate[:, span].astype(jnp.float32))
            value = lin[:, span] * enter_all[...] * gain_ref[:, span] * opened
            made.append((span, value.astype(jnp.bfloat16)))
        for span, value in made:
            lin_stage[:, span] = value
        return carry

    lax.fori_loop(0, heads // 4, finish_lin, 0)
    lin_store = pltpu.make_async_copy(lin_stage, lin_hbm, out_sem.at[1])
    lin_store.start()
    for distance in range(1, window + 1):

        @pl.when(sends(distance))
        def drain():
            for copy in far_copies(distance):
                copy.wait_send()

    for step in range(1, head_size):
        square_copy(step).wait_send()
    soft_store.wait()
    lin_store.wait()


def per_device(
    lin_query,
    lin_key,
    lin_value,
    lin_gate,
    lin_decay,
    norm_gain,
    soft_query,
    soft_key,
    soft_value,
    starts,
    lengths,
):
    rows, features = lin_query.shape
    kv_features = soft_key.shape[1]
    heads = features // TILE
    ctx_size, head_size = lax.axis_size("ctx"), lax.axis_size("head")
    window = ctx_size // starts.shape[0]
    f32, bf16 = jnp.float32, jnp.bfloat16
    anywhere = pl.BlockSpec(memory_space=pl.ANY)
    vmem = pl.BlockSpec(memory_space=pltpu.VMEM)
    smem = pl.BlockSpec(memory_space=pltpu.SMEM)
    wide = pltpu.VMEM((rows, features), bf16)
    narrow = pltpu.VMEM((rows, kv_features), bf16)
    dma = pltpu.SemaphoreType.DMA
    scratch = [wide, wide, wide, wide, wide, narrow, narrow]
    scratch += [
        pltpu.VMEM((window, rows, kv_features), bf16),
        pltpu.VMEM((window, rows, kv_features), bf16),
        pltpu.VMEM((heads, TILE, TILE), bf16),
        pltpu.VMEM((window, heads, TILE, TILE), bf16),
        pltpu.VMEM((heads, TILE), f32),
        pltpu.VMEM((window, heads, TILE), f32),
        pltpu.VMEM((TILE, rows), f32),
        pltpu.VMEM((rows, TILE), f32),
        pltpu.VMEM((rows, TILE), f32),
        pltpu.VMEM((rows, TILE), f32),
        pltpu.VMEM((rows, TILE), f32),
        pltpu.VMEM((window + 1, rows, rows), f32),
        pltpu.VMEM((rows, features), f32),
        pltpu.VMEM((8, rows), f32),
        pltpu.VMEM((head_size - 1, 8, rows), f32),
        wide,
        wide,
        dma((7,)),
        dma((2,)),
        dma((window, 2)),
        dma((window, 2)),
        dma((window, PARTS + 1)),
        dma((window, PARTS + 1)),
        dma((head_size - 1,)),
        dma((head_size - 1,)),
    ]
    out = jax.ShapeDtypeStruct((rows, features), bf16)
    return pl.pallas_call(
        functools.partial(kernel, ctx_size, head_size),
        out_shape=(out, out),
        in_specs=[anywhere] * 4 + [vmem, vmem] + [anywhere] * 3 + [smem, smem],
        out_specs=(anywhere, anywhere),
        scratch_shapes=scratch,
        compiler_params=pltpu.CompilerParams(
            collective_id=0, has_side_effects=True, vmem_limit_bytes=56 * 1024 * 1024
        ),
    )(
        lin_query,
        lin_key,
        lin_value,
        lin_gate,
        lin_decay.T,
        norm_gain.reshape(1, features),
        soft_query,
        soft_key,
        soft_value,
        starts,
        lengths,
    )


def solution(mesh):
    both = P("ctx", "head")
    placed = (both, both, both, both, both, P("head"), both, both, both, P(), P())
    return jax.shard_map(
        per_device, mesh=mesh, in_specs=placed, out_specs=(both, both), check_vma=False
    )
```
